512 devices in a mesh: aux: 64 (over y, x, z_lo), basis: 8 (over z_hi, core).
Axes of the slice: x: 4, y: 8, z: 8 (z_hi: 4, z_lo: 2; z = z_hi * 2 + z_lo), core: 2. Of those that a mesh axis runs over, the one named last changes fastest.
Arguments:
- integrals: float32 [128, 512, 4096], P('aux', None, 'basis'), may hold values from -0.75 to 0.75
- occupied: float32 [4096, 768], P('basis', 'aux'), may hold values from -0.09375 to 0.09375
Outputs:
- exchange: float32 [256, 256], P('aux', 'basis')
The draws below stay inside these ranges and needn't reach their ends.
All inputs are finite; a program needn't handle non-finite values.
Results may differ from the reference program's by a relative error of at most 0.000078.
Values sent between devices are 32-bit elements; how exact they have to be, the bound alone decides.
No kernel may reach another device: no remote copies, remote signals or barrier semaphores. Data moves between devices by JAX's collectives and lax.ppermute only.
A program may use at most 64 MiB of HBM per device.

```python
import jax
import jax.numpy as jnp
from jax import lax

NB = 4096
NOCC = 768
HALF = 256
AUX = 128
N_AUX = 64


def spiked(entries, rng, source, target, shards_of, factor):
    owner, partner = [(jnp.arange(entries.shape[position]) // (entries.shape[position] // shards_of)).reshape([-1 if axis == position else 1 for axis in range(entries.ndim)]) for position in (source, target)]
    chosen = jax.random.permutation(rng, shards_of)[partner]
    strong = (owner == chosen) | (owner == (partner + shards_of // 2) % shards_of)
    return jnp.where(strong, factor * entries, entries)


def steps_of(own_key, shape, shards, smallest, high):
    gain, own = 1.0, jax.random.fold_in(own_key, 6)
    for position, shards_of in shards:
        heights = jnp.exp(jax.random.uniform(jax.random.fold_in(own, position), (shards_of,), jnp.float32, smallest / len(shards), high / len(shards)))
        gain = gain * jnp.repeat(heights, shape[position] // shards_of).reshape([-1 if axis == position else 1 for axis in range(len(shape))])
    return gain


def gaussian(rng, extent, width, limit, split=(), kind=jnp.bfloat16):
    drawn = width * jax.random.normal(rng, extent, jnp.float32)
    if split:
        drawn = drawn * steps_of(rng, extent, split, -0.22, 0.18)
    return jnp.clip(drawn, -limit, limit).astype(kind)


def bell_draw_with(rng, shape, scale, most, shards, heavy, held_as=jnp.bfloat16):
    entries = scale * jax.random.normal(rng, shape, jnp.float32)
    if shards:
        entries = entries * steps_of(rng, shape, shards, -0.22, 0.18)
    return jnp.clip(spiked(entries, jax.random.fold_in(rng, 3), *heavy), -most, most).astype(held_as)


def setup_inputs(seed: int = 0) -> dict:
    arg_keys = jax.random.split(jax.random.key(seed), 3)
    integrals = bell_draw_with(arg_keys[0], (AUX, 2 * HALF, NB), (8 * N_AUX) ** -0.5, 0.75, ((0, 64), (2, 8)), (0, 1, 64, 4.0), jnp.float32)
    occupied = gaussian(arg_keys[1], (NB, NOCC), NB ** -0.5, 0.09375, ((0, 8), (1, 64)), jnp.float32)
    return {"integrals": integrals, "occupied": occupied}


def reference(integrals, occupied):
    transformed = jnp.einsum("prl,li->pri", integrals, occupied, precision=lax.Precision.HIGHEST)
    return jnp.einsum("pmi,pni->mn", transformed[:, :HALF], transformed[:, HALF:], precision=lax.Precision.HIGHEST)
```

```python
import jax
import jax.numpy as jnp
from jax import lax
from jax.sharding import Mesh
from jax.sharding import PartitionSpec as P

Y, X, ZL, ZH, C = 8, 4, 2, 4, 2


def spread(block, axes, count):
    return lax.all_to_all(
        jnp.broadcast_to(block, (count,) + block.shape), axes, 0, 0, tiled=True
    )


def body(integrals, occupied):
    parts, rows, depth = integrals.shape
    own = occupied.shape[1]
    half = rows // 2
    swapped = lax.ppermute(integrals, "c", [(0, 1), (1, 0)])
    core = lax.axis_index("c")
    low = jnp.where(core == 0, integrals, swapped)
    high = jnp.where(core == 0, swapped, integrals)

    coefficients = occupied.T.reshape(C, own // C, depth)
    sent = jnp.broadcast_to(coefficients, (Y, ZL) + coefficients.shape)
    sent = sent.reshape(Y * ZL * C, own // C, depth)
    near = lax.all_to_all(sent, ("y", "zl", "c"), 0, 0, tiled=True)
    whole = spread(near, "x", X)
    whole = whole.reshape(X * Y * ZL, C, own // C, depth)

    def term(block, c):
        return jnp.einsum(
            "gil,prl->gipr", whole[:, c], block, precision=lax.Precision.HIGH
        )

    partial_x = term(low, 0) + term(high, 1)
    orbitals = X * Y * ZL * own // C
    partial_x = partial_x.reshape(ZH, orbitals // ZH, parts, rows)
    arrived = lax.all_to_all(partial_x, "zh", 0, 0, tiled=True)
    summed = jnp.sum(arrived, axis=0)
    tile = jnp.einsum(
        "ipm,ipn->mn", summed[:, :, :half], summed[:, :, half:], precision=lax.Precision.HIGH
    )

    m, n = half // (Y * X * ZL), half // (ZH * C)
    tile = tile.reshape(Y, X, ZL, m, ZH, C, n).transpose(1, 2, 5, 0, 4, 3, 6)
    tile = lax.all_to_all(
        tile.reshape(X * ZL * C, Y, ZH, m, n), ("x", "zl", "c"), 0, 0, tiled=True
    )
    tile = jnp.sum(tile, axis=0).reshape(Y * ZH, m, n)
    tile = lax.all_to_all(tile, ("y", "zh"), 0, 0, tiled=True)
    return jnp.sum(tile, axis=0)


def solution(mesh):
    refined = Mesh(mesh.devices.reshape(Y, X, ZL, ZH, C), ("y", "x", "zl", "zh", "c"))
    aux, basis = ("y", "x", "zl"), ("zh", "c")
    return jax.shard_map(
        body,
        mesh=refined,
        in_specs=(P(aux, None, basis), P(basis, aux)),
        out_specs=P(aux, basis),
        check_vma=False,
    )
```

```python
import jax
import jax.numpy as jnp
from jax import lax
from jax.sharding import Mesh
from jax.sharding import PartitionSpec as P

Y, X, ZL, ZH, C = 8, 4, 2, 4, 2
LANES = 128


def body(integrals, occupied):
    parts, rows, depth = integrals.shape
    own = occupied.shape[1]
    half = rows // 2
    share = own // C
    swapped = lax.ppermute(integrals, "c", [(0, 1), (1, 0)])
    held = jnp.concatenate([integrals, swapped], axis=2).reshape(parts * rows, C * depth)

    sent = jnp.broadcast_to(
        occupied.T.reshape(C, share * depth // LANES, LANES),
        (Y, C, share * depth // LANES, LANES),
    )
    near = lax.all_to_all(
        sent.reshape(Y * C, -1, LANES), ("y", "c"), 0, 0, tiled=True
    ).reshape(Y, C, share, depth)
    near = jnp.where(lax.axis_index("c") == 0, near, near[:, ::-1])
    near = near.transpose(0, 2, 1, 3).reshape(Y * share, C * depth)
    whole = lax.all_to_all(
        jnp.broadcast_to(near, (X * ZL,) + near.shape), ("x", "zl"), 0, 0, tiled=True
    )
    whole = whole.reshape(-1, C * depth)

    partial_x = lax.dot_general(
        whole, held, (((1,), (1,)), ((), ())), precision=lax.Precision.HIGH
    )
    orbitals = partial_x.shape[0] // ZH
    arrived = lax.all_to_all(
        partial_x.reshape(ZH, orbitals, parts * rows), "zh", 0, 0, tiled=True
    )
    summed = jnp.sum(arrived, axis=0)
    tile = sum(
        lax.dot_general(
            summed[:, p * rows : p * rows + half],
            summed[:, p * rows + half : (p + 1) * rows],
            (((0,), (0,)), ((), ())),
            precision=lax.Precision.HIGHEST,
        )
        for p in range(parts)
    )

    m, n = half // (Y * X * ZL), half // (ZH * C)
    tile = lax.all_to_all(tile.reshape(Y * X, ZL * m, half), ("y", "x"), 0, 0, tiled=True)
    tile = jnp.sum(tile, axis=0).reshape(ZL, m, ZH * C, n).transpose(0, 2, 1, 3)
    tile = lax.all_to_all(
        tile.reshape(ZL * ZH * C, m * n), ("zl", "zh", "c"), 0, 0, tiled=True
    )
    return jnp.sum(tile, axis=0).reshape(m, n)


def solution(mesh):
    refined = Mesh(mesh.devices.reshape(Y, X, ZL, ZH, C), ("y", "x", "zl", "zh", "c"))
    aux, basis = ("y", "x", "zl"), ("zh", "c")
    return jax.shard_map(
        body,
        mesh=refined,
        in_specs=(P(aux, None, basis), P(basis, aux)),
        out_specs=P(aux, basis),
        check_vma=False,
    )
```

```python
import jax
import jax.numpy as jnp
from jax import lax
from jax.sharding import Mesh
from jax.sharding import PartitionSpec as P

Y, X, ZL, ZH, C = 8, 4, 2, 4, 2
LANES = 128


def body(integrals, occupied):
    parts, rows, depth = integrals.shape
    own = occupied.shape[1]
    half = rows // 2
    share = own // C
    swapped = lax.ppermute(integrals, "c", [(0, 1), (1, 0)])
    held = jnp.concatenate([integrals, swapped], axis=2).reshape(parts * rows, C * depth)

    pairs = [((x + d + 2) % X * ZH + d, x * ZH + d) for x in range(X) for d in range(ZH)]
    moved = lax.ppermute(occupied.T, ("x", "zh"), pairs)
    sent = jnp.broadcast_to(
        moved.reshape(C, share * depth // LANES, LANES),
        (Y, ZL, C, share * depth // LANES, LANES),
    )
    near = lax.all_to_all(
        sent.reshape(Y * ZL * C, -1, LANES), ("y", "zl", "c"), 0, 0, tiled=True
    ).reshape(Y * ZL, C, share, depth)
    near = jnp.where(lax.axis_index("c") == 0, near, near[:, ::-1])
    near = near.transpose(0, 2, 1, 3).reshape(Y * ZL * share, C * depth)

    def fetch(source, step):
        return lax.ppermute(source, "x", [((x + step) % X, x) for x in range(X)])

    def term(block):
        return lax.dot_general(
            block, held, (((1,), (1,)), ((), ())), precision=lax.Precision.HIGH
        )

    up = [(d, (d + 1) % ZH) for d in range(ZH)]
    down = [(d, (d - 1) % ZH) for d in range(ZH)]
    next_one, last_one = fetch(near, -1), fetch(near, 1)
    opposite = term(near)
    cut = opposite.shape[0] // 2
    from_below = lax.ppermute(opposite[:cut], "zh", up)
    from_above = lax.ppermute(opposite[cut:], "zh", down)
    above, below = term(next_one), term(last_one)
    near, above = lax.optimization_barrier((near, above))
    arrived_up = lax.ppermute(
        jnp.concatenate([above[:cut] + from_below, above[cut:]]), "zh", up
    )
    arrived_down = lax.ppermute(
        jnp.concatenate([below[:cut], below[cut:] + from_above]), "zh", down
    )
    mine = lax.optimization_barrier(term(fetch(near, 2)))
    summed = mine + arrived_up + arrived_down
    tile = sum(
        lax.dot_general(
            summed[:, p * rows : p * rows + half],
            summed[:, p * rows + half : (p + 1) * rows],
            (((0,), (0,)), ((), ())),
            precision=lax.Precision.HIGHEST,
        )
        for p in range(parts)
    )

    m, n = half // (Y * X * ZL), half // (ZH * C)
    tile = lax.all_to_all(tile.reshape(Y * X, ZL * m, half), ("y", "x"), 0, 0, tiled=True)
    tile = jnp.sum(tile, axis=0).reshape(ZL, m, ZH * C, n).transpose(0, 2, 1, 3)
    tile = lax.all_to_all(
        tile.reshape(ZL * ZH * C, m * n), ("zl", "zh", "c"), 0, 0, tiled=True
    )
    return jnp.sum(tile, axis=0).reshape(m, n)


def solution(mesh):
    refined = Mesh(mesh.devices.reshape(Y, X, ZL, ZH, C), ("y", "x", "zl", "zh", "c"))
    aux, basis = ("y", "x", "zl"), ("zh", "c")
    return jax.shard_map(
        body,
        mesh=refined,
        in_specs=(P(aux, None, basis), P(basis, aux)),
        out_specs=P(aux, basis),
        check_vma=False,
    )
```

```python
import itertools

import jax
import jax.numpy as jnp
from jax import lax
from jax.sharding import Mesh
from jax.sharding import PartitionSpec as P

Y, X, ZL, ZH, C = 8, 4, 2, 4, 2
LANES = 128


def body(integrals, occupied):
    parts, rows, depth = integrals.shape
    own = occupied.shape[1]
    half = rows // 2
    share = own // C
    swapped = lax.ppermute(integrals, "c", [(0, 1), (1, 0)])
    held = jnp.concatenate([integrals, swapped], axis=2).reshape(parts * rows, C * depth)

    pairs = [((x + d + 2) % X * ZH + d, x * ZH + d) for x in range(X) for d in range(ZH)]
    moved = lax.ppermute(occupied.T, ("x", "zh"), pairs)
    sent = jnp.broadcast_to(
        moved.reshape(C, share * depth // LANES, LANES),
        (Y, ZL, C, share * depth // LANES, LANES),
    )
    near = lax.all_to_all(
        sent.reshape(Y * ZL * C, -1, LANES), ("y", "zl", "c"), 0, 0, tiled=True
    ).reshape(Y * ZL, C, share, depth)
    near = jnp.where(lax.axis_index("c") == 0, near, near[:, ::-1])
    near = near.transpose(0, 2, 1, 3).reshape(Y * ZL * share, C * depth)

    def paired(block, pairing):
        target = lambda d, c: (d + (1 if (d + c + pairing) % 2 == 0 else -1)) % ZH
        pairs = [(d * C + c, target(d, c) * C + c) for d in range(ZH) for c in range(C)]
        return lax.ppermute(block, ("zh", "c"), pairs)

    def fetch(source, pairing):
        pairs = []
        for x, d, c in itertools.product(range(X), range(ZH), range(C)):
            step = -1 if (d + c + pairing) % 2 == 0 else 1
            pairs.append((((x + step) % X * ZH + d) * C + c, (x * ZH + d) * C + c))
        return lax.ppermute(source, ("x", "zh", "c"), pairs)

    def term(block):
        return lax.dot_general(
            block, held, (((1,), (1,)), ((), ())), precision=lax.Precision.HIGH
        )

    block_a, block_b = fetch(near, 0), fetch(near, 1)
    passed = paired(term(near), 0)
    term_a = term(block_a)
    from_a = paired(term_a, 0)
    near, term_a = lax.optimization_barrier((near, term_a))
    from_a, sent_b = lax.optimization_barrier((from_a, term(block_b) + passed))
    from_b = paired(sent_b, 1)
    block = lax.ppermute(near, "x", [((x + 2) % X, x) for x in range(X)])
    mine = lax.optimization_barrier(term(block))
    summed = mine + from_a + from_b
    tile = sum(
        lax.dot_general(
            summed[:, p * rows : p * rows + half],
            summed[:, p * rows + half : (p + 1) * rows],
            (((0,), (0,)), ((), ())),
            precision=lax.Precision.HIGHEST,
        )
        for p in range(parts)
    )

    m, n = half // (Y * X * ZL), half // (ZH * C)
    tile = lax.all_to_all(tile.reshape(Y * X, ZL * m, half), ("y", "x"), 0, 0, tiled=True)
    tile = jnp.sum(tile, axis=0).reshape(ZL, m, ZH * C, n).transpose(0, 2, 1, 3)
    tile = lax.all_to_all(
        tile.reshape(ZL * ZH * C, m * n), ("zl", "zh", "c"), 0, 0, tiled=True
    )
    return jnp.sum(tile, axis=0).reshape(m, n)


def solution(mesh):
    refined = Mesh(mesh.devices.reshape(Y, X, ZL, ZH, C), ("y", "x", "zl", "zh", "c"))
    aux, basis = ("y", "x", "zl"), ("zh", "c")
    return jax.shard_map(
        body,
        mesh=refined,
        in_specs=(P(aux, None, basis), P(basis, aux)),
        out_specs=P(aux, basis),
        check_vma=False,
    )
```

```python
import itertools

import jax
import jax.numpy as jnp
from jax import lax
from jax.sharding import Mesh
from jax.sharding import PartitionSpec as P

Y, X, ZL, ZH, C = 8, 4, 2, 4, 2
LANES = 128


def body(integrals, occupied):
    parts, rows, depth = integrals.shape
    own = occupied.shape[1]
    half = rows // 2
    share = own // C
    swapped = lax.ppermute(integrals, "c", [(0, 1), (1, 0)])
    held = jnp.concatenate([integrals, swapped], axis=2).reshape(parts * rows, C * depth)

    pairs = [((x + d + 2) % X * ZH + d, x * ZH + d) for x in range(X) for d in range(ZH)]
    moved = lax.ppermute(occupied.T, ("x", "zh"), pairs)
    sent = jnp.broadcast_to(
        moved.reshape(C, share * depth // LANES, LANES),
        (Y, ZL, C, share * depth // LANES, LANES),
    )
    near = lax.all_to_all(
        sent.reshape(Y * ZL * C, -1, LANES), ("y", "zl", "c"), 0, 0, tiled=True
    ).reshape(Y * ZL, C, share, depth)
    near = jnp.where(lax.axis_index("c") == 0, near, near[:, ::-1])
    near = near.transpose(0, 2, 1, 3).reshape(Y * ZL * share, C * depth)

    def paired(block, pairing):
        target = lambda d, c: (d + (1 if (d + c + pairing) % 2 == 0 else -1)) % ZH
        pairs = [(d * C + c, target(d, c) * C + c) for d in range(ZH) for c in range(C)]
        return lax.ppermute(block, ("zh", "c"), pairs)

    def fetch(source, pairing):
        pairs = []
        for x, d, c in itertools.product(range(X), range(ZH), range(C)):
            step = -1 if (d + c + pairing) % 2 == 0 else 1
            pairs.append((((x + step) % X * ZH + d) * C + c, (x * ZH + d) * C + c))
        return lax.ppermute(source, ("x", "zh", "c"), pairs)

    def term(block):
        return lax.dot_general(
            block, held, (((1,), (1,)), ((), ())), precision=lax.Precision.HIGH
        )

    block_a, block_b = fetch(near, 0), fetch(near, 1)
    passed = paired(term(near), 0)
    term_a = term(block_a)
    cut = term_a.shape[0] // 2
    from_a, later_a = paired(term_a[:cut], 0), paired(term_a[cut:], 0)
    near, term_a = lax.optimization_barrier((near, term_a))
    from_a, sent_b = lax.optimization_barrier((from_a, term(block_b) + passed))
    from_b = paired(sent_b, 1)
    block = lax.ppermute(near, "x", [((x + 2) % X, x) for x in range(X)])
    mine = lax.optimization_barrier(term(block))
    summed = mine + jnp.concatenate([from_a, later_a]) + from_b
    tile = sum(
        lax.dot_general(
            summed[:, p * rows : p * rows + half],
            summed[:, p * rows + half : (p + 1) * rows],
            (((0,), (0,)), ((), ())),
            precision=lax.Precision.HIGHEST,
        )
        for p in range(parts)
    )

    m, n = half // (Y * X * ZL), half // (ZH * C)
    tile = lax.all_to_all(tile.reshape(Y * X, ZL * m, half), ("y", "x"), 0, 0, tiled=True)
    tile = jnp.sum(tile, axis=0).reshape(ZL, m, ZH * C, n).transpose(0, 2, 1, 3)
    tile = lax.all_to_all(
        tile.reshape(ZL * ZH * C, m * n), ("zl", "zh", "c"), 0, 0, tiled=True
    )
    return jnp.sum(tile, axis=0).reshape(m, n)


def solution(mesh):
    refined = Mesh(mesh.devices.reshape(Y, X, ZL, ZH, C), ("y", "x", "zl", "zh", "c"))
    aux, basis = ("y", "x", "zl"), ("zh", "c")
    return jax.shard_map(
        body,
        mesh=refined,
        in_specs=(P(aux, None, basis), P(basis, aux)),
        out_specs=P(aux, basis),
        check_vma=False,
    )
```

```python
import itertools

import jax
import jax.numpy as jnp
from jax import lax
from jax.sharding import Mesh
from jax.sharding import PartitionSpec as P

Y, X, ZL, ZH, C = 8, 4, 2, 4, 2
LANES = 128


def body(integrals, occupied):
    parts, rows, depth = integrals.shape
    own = occupied.shape[1]
    half = rows // 2
    share = own // C
    swapped = lax.ppermute(integrals, "c", [(0, 1), (1, 0)])
    held = jnp.concatenate([integrals, swapped], axis=2).reshape(parts * rows, C * depth)

    pairs = [((x + d + 2) % X * ZH + d, x * ZH + d) for x in range(X) for d in range(ZH)]
    moved = lax.ppermute(occupied.T, ("x", "zh"), pairs)
    sent = jnp.broadcast_to(
        moved.reshape(C, share * depth // LANES, LANES),
        (Y, ZL, C, share * depth // LANES, LANES),
    )
    near = lax.all_to_all(
        sent.reshape(Y * ZL * C, -1, LANES), ("y", "zl", "c"), 0, 0, tiled=True
    ).reshape(Y * ZL, C, share, depth)
    near = jnp.where(lax.axis_index("c") == 0, near, near[:, ::-1])
    near = near.transpose(0, 2, 1, 3).reshape(Y * ZL * share, C * depth)

    def paired(block, pairing):
        target = lambda d, c: (d + (1 if (d + c + pairing) % 2 == 0 else -1)) % ZH
        pairs = [(d * C + c, target(d, c) * C + c) for d in range(ZH) for c in range(C)]
        return lax.ppermute(block, ("zh", "c"), pairs)

    def fetch(source, pairing):
        pairs = []
        for x, d, c in itertools.product(range(X), range(ZH), range(C)):
            step = -1 if (d + c + pairing) % 2 == 0 else 1
            pairs.append((((x + step) % X * ZH + d) * C + c, (x * ZH + d) * C + c))
        return lax.ppermute(source, ("x", "zh", "c"), pairs)

    def term(block):
        return lax.dot_general(
            block, held, (((1,), (1,)), ((), ())), precision=lax.Precision.HIGH
        )

    block_a, block_b = fetch(near, 0), fetch(near, 1)
    passed = paired(term(near), 0)
    term_a = term(block_a)
    cut = term_a.shape[0] // 2
    from_a, later_a = paired(term_a[:cut], 0), paired(term_a[cut:], 0)
    near, term_a = lax.optimization_barrier((near, term_a))
    term_b = lax.optimization_barrier(term(block_b))
    from_a, sent_b = lax.optimization_barrier((from_a, term_b + passed))
    from_b = paired(sent_b, 1)
    block = lax.ppermute(near, "x", [((x + 2) % X, x) for x in range(X)])
    mine = lax.optimization_barrier(term(block))
    summed = mine + jnp.concatenate([from_a, later_a]) + from_b
    tile = sum(
        lax.dot_general(
            summed[:, p * rows : p * rows + half],
            summed[:, p * rows + half : (p + 1) * rows],
            (((0,), (0,)), ((), ())),
            precision=lax.Precision.HIGHEST,
        )
        for p in range(parts)
    )

    m, n = half // (Y * X * ZL), half // (ZH * C)
    tile = lax.all_to_all(tile.reshape(Y * X, ZL * m, half), ("y", "x"), 0, 0, tiled=True)
    tile = jnp.sum(tile, axis=0).reshape(ZL, m, ZH * C, n).transpose(0, 2, 1, 3)
    tile = lax.all_to_all(
        tile.reshape(ZL * ZH * C, m * n), ("zl", "zh", "c"), 0, 0, tiled=True
    )
    return jnp.sum(tile, axis=0).reshape(m, n)


def solution(mesh):
    refined = Mesh(mesh.devices.reshape(Y, X, ZL, ZH, C), ("y", "x", "zl", "zh", "c"))
    aux, basis = ("y", "x", "zl"), ("zh", "c")
    return jax.shard_map(
        body,
        mesh=refined,
        in_specs=(P(aux, None, basis), P(basis, aux)),
        out_specs=P(aux, basis),
        check_vma=False,
    )
```

```python
import itertools

import jax
import jax.numpy as jnp
from jax import lax
from jax.sharding import Mesh
from jax.sharding import PartitionSpec as P

Y, X, ZL, ZH, C = 8, 4, 2, 4, 2
LANES = 128


def body(integrals, occupied):
    parts, rows, depth = integrals.shape
    own = occupied.shape[1]
    half = rows // 2
    share = own // C
    pairs = [((x + d + 2) % X * ZH + d, x * ZH + d) for x in range(X) for d in range(ZH)]
    moved = lax.ppermute(occupied.T, ("x", "zh"), pairs)
    swapped = lax.ppermute(integrals, "c", [(0, 1), (1, 0)])
    held = jnp.concatenate([integrals, swapped], axis=2).reshape(parts * rows, C * depth)
    sent = jnp.broadcast_to(
        moved.reshape(C, share * depth // LANES, LANES),
        (Y, ZL, C, share * depth // LANES, LANES),
    )
    near = lax.all_to_all(
        sent.reshape(Y * ZL * C, -1, LANES), ("y", "zl", "c"), 0, 0, tiled=True
    ).reshape(Y * ZL, C, share, depth)
    near = jnp.where(lax.axis_index("c") == 0, near, near[:, ::-1])
    near = near.transpose(0, 2, 1, 3).reshape(Y * ZL * share, C * depth)

    def paired(block, pairing):
        target = lambda d, c: (d + (1 if (d + c + pairing) % 2 == 0 else -1)) % ZH
        pairs = [(d * C + c, target(d, c) * C + c) for d in range(ZH) for c in range(C)]
        return lax.ppermute(block, ("zh", "c"), pairs)

    def fetch(source, pairing):
        pairs = []
        for x, d, c in itertools.product(range(X), range(ZH), range(C)):
            step = -1 if (d + c + pairing) % 2 == 0 else 1
            pairs.append((((x + step) % X * ZH + d) * C + c, (x * ZH + d) * C + c))
        return lax.ppermute(source, ("x", "zh", "c"), pairs)

    def term(block):
        return lax.dot_general(
            block, held, (((1,), (1,)), ((), ())), precision=lax.Precision.HIGH
        )

    block_a, block_b = fetch(near, 0), fetch(near, 1)
    passed = paired(term(near), 0)
    term_a = term(block_a)
    from_a = paired(term_a, 0)
    near, term_a = lax.optimization_barrier((near, term_a))
    from_a, sent_b = lax.optimization_barrier((from_a, term(block_b) + passed))
    from_b = paired(sent_b, 1)
    block = lax.ppermute(near, "x", [((x + 2) % X, x) for x in range(X)])
    mine = lax.optimization_barrier(term(block))
    summed = mine + from_a + from_b
    tile = sum(
        lax.dot_general(
            summed[:, p * rows : p * rows + half],
            summed[:, p * rows + half : (p + 1) * rows],
            (((0,), (0,)), ((), ())),
            precision=lax.Precision.HIGHEST,
        )
        for p in range(parts)
    )

    m, n = half // (Y * X * ZL), half // (ZH * C)
    tile = lax.all_to_all(tile.reshape(Y * X, ZL * m, half), ("y", "x"), 0, 0, tiled=True)
    tile = jnp.sum(tile, axis=0).reshape(ZL, m, ZH * C, n).transpose(0, 2, 1, 3)
    tile = lax.all_to_all(
        tile.reshape(ZL * ZH * C, m * n), ("zl", "zh", "c"), 0, 0, tiled=True
    )
    return jnp.sum(tile, axis=0).reshape(m, n)


def solution(mesh):
    refined = Mesh(mesh.devices.reshape(Y, X, ZL, ZH, C), ("y", "x", "zl", "zh", "c"))
    aux, basis = ("y", "x", "zl"), ("zh", "c")
    return jax.shard_map(
        body,
        mesh=refined,
        in_specs=(P(aux, None, basis), P(basis, aux)),
        out_specs=P(aux, basis),
        check_vma=False,
    )
```
